32 devices in a mesh: qrow: 8 (over z, core), kcol: 4 (over y, x).
Axes of the slice: x: 2, y: 2, z: 4, core: 2. Of those that a mesh axis runs over, the one named last changes fastest.
Arguments:
- query_rows: bfloat16 [4096, 512], P(('qrow', 'kcol')), may hold values from -6 to 6
- key_rows: bfloat16 [4096, 512], P(('kcol', 'qrow')), may hold values from -6 to 6
- value_rows: bfloat16 [4096, 512], P(('kcol', 'qrow')), may hold values from -6 to 6
- layer_out: bfloat16 [4096, 512], P(('qrow', 'kcol')), may hold values from -6 to 6
- grad_out: bfloat16 [4096, 512], P(('qrow', 'kcol')), may hold values from -6 to 6
- block_order: int32 [32], replicated, may hold values from 0 to 31, each once
- tile_mask: int32 [32, 32], replicated, may hold values from 0 to 1, as said below
Outputs:
- grad_query: float32 [4096, 512], P(('qrow', 'kcol'))
- grad_key: float32 [4096, 512], P(('kcol', 'qrow'))
- grad_value: float32 [4096, 512], P(('kcol', 'qrow'))
The draws below stay inside these ranges and needn't reach their ends.
Inputs may be any that keep to these rules, and one draw needn't show every extreme that they name: block_order is a permutation of 0 to 31. tile_mask[a, b] is 1 exactly where logical blocks a and b lie in the same document and b <= a, where documents are runs of consecutive logical blocks; the diagonal is 1.
All inputs are finite; a program needn't handle non-finite values.
Results may differ from the reference program's by a relative error of at most 0.0035.
Values may be sent and summed in bfloat16 or wider, within the bound.
A program may use at most 192 MiB of HBM per device.

```python
import math
import jax
import jax.numpy as jnp
from jax import lax

HD = 128
H = 4
BLOCK = 128
BLOCKS = 32
TOKENS = 4096
HDIM = 512


def draw_query_rows(key, part):
    key = jax.random.fold_in(key, 1)
    base = jnp.clip(jax.random.normal(key, (TOKENS, HDIM), jnp.float32), -4.5, 4.5)
    return base.astype(jnp.bfloat16)


def draw_key_rows(key, part):
    key = jax.random.fold_in(key, 2)
    base = jnp.clip(jax.random.normal(key, (TOKENS, HDIM), jnp.float32), -4.5, 4.5)
    return base.astype(jnp.bfloat16)


def draw_tile_mask(key, part):
    key = jax.random.fold_in(key, 5)
    labels = jnp.arange(BLOCKS, dtype=jnp.int32)
    starts = (jax.random.randint(key, (BLOCKS,), 0, 24) == 0) | (labels == 0)
    document = jnp.cumsum(starts.astype(jnp.int32))
    allowed = (document[:, None] == document[None, :]) & (labels[None, :] <= labels[:, None])
    return allowed.astype(jnp.int32)


def block_levels(own_key, dims, shards, least, high):
    level = 1.0
    for dim, parts in shards:
        heights = jax.random.uniform(jax.random.fold_in(jax.random.fold_in(own_key, 6), dim), (parts,), jnp.float32, least / len(shards), high / len(shards))
        level = level * jnp.repeat(jnp.exp(heights), dims[dim] // parts).reshape((-1,) + (1,) * (len(dims) - 1 - dim))
    return level


def scatter_about(rng, dims, deviation, most, split=(), held_as=jnp.bfloat16):
    drawn = jax.random.normal(rng, dims, jnp.float32) * deviation
    if len(split) > 0:
        drawn = block_levels(rng, dims, split, -0.22, 0.18) * drawn
    return jnp.clip(drawn, min=-most, max=most).astype(held_as)


def setup_inputs(seed: int = 0) -> dict:
    key_of = jax.random.split(jax.random.key(seed), 8)
    query_rows = draw_query_rows(jax.random.fold_in(key_of[7], 71), 0)
    key_rows = draw_key_rows(jax.random.fold_in(key_of[7], 71), 0)
    value_rows = scatter_about(key_of[2], (TOKENS, HDIM), 1.0, 6.0, ((0, 32),))
    layer_out = scatter_about(key_of[3], (TOKENS, HDIM), 1.0, 6.0, ((0, 32),))
    grad_out = scatter_about(key_of[4], (TOKENS, HDIM), 1.0, 6.0, ((0, 32),))
    block_order = jax.random.permutation(key_of[5], BLOCKS).astype(jnp.int32)
    tile_mask = draw_tile_mask(jax.random.fold_in(key_of[7], 71), 0)
    return dict(query_rows=query_rows, key_rows=key_rows, value_rows=value_rows, layer_out=layer_out, grad_out=grad_out, block_order=block_order, tile_mask=tile_mask)


def reference(query_rows, key_rows, value_rows, layer_out, grad_out, block_order, tile_mask):
    score_scale = 1.0 / math.sqrt(HD)
    logical = jnp.repeat(block_order.astype(jnp.int32), BLOCK)
    offsets = jnp.arange(TOKENS, dtype=jnp.int32) % BLOCK
    position = logical * BLOCK + offsets
    products = (grad_out.astype(jnp.float32) * layer_out.astype(jnp.float32)).reshape(TOKENS, H, HD)
    delta = lax.optimization_barrier(lax.optimization_barrier(jnp.sum(products, axis=2)).astype(jnp.bfloat16)).astype(jnp.float32)
    key_heads = key_rows.astype(jnp.float32).reshape(TOKENS, H, HD)
    value_heads = value_rows.astype(jnp.float32).reshape(TOKENS, H, HD)
    span = BLOCK * 4
    count = TOKENS // span

    def one_step(carry, step_number):
        key_total, value_total = carry
        start = (step_number * span).astype(jnp.int32)
        query_block = lax.dynamic_slice_in_dim(query_rows, start, span, 0).astype(jnp.float32).reshape(span, H, HD)
        grad_block = lax.dynamic_slice_in_dim(grad_out, start, span, 0).astype(jnp.float32).reshape(span, H, HD)
        delta_block = lax.dynamic_slice_in_dim(delta, start, span, 0)
        logical_block = lax.dynamic_slice_in_dim(logical, start, span, 0)
        position_block = lax.dynamic_slice_in_dim(position, start, span, 0)
        mask_rows = jnp.take(tile_mask, logical_block, axis=0)
        allowed = (jnp.take(mask_rows, logical, axis=1) == 1) & (position[None, :] <= position_block[:, None])
        scores = jnp.einsum('qhd,khd->hqk', query_block, key_heads) * score_scale
        scores = jnp.where(allowed[None], scores, -jnp.inf)
        largest = lax.optimization_barrier(jnp.max(scores, axis=2, keepdims=True))
        log_totals = largest + jnp.log(lax.optimization_barrier(jnp.sum(jnp.exp(scores - largest), axis=2, keepdims=True)))
        probs = jnp.exp(scores - log_totals)
        probs_low = lax.optimization_barrier(probs.astype(jnp.bfloat16)).astype(jnp.float32)
        dprobs = jnp.einsum('qhd,khd->hqk', grad_block, value_heads)
        dscores = probs * (dprobs - jnp.transpose(delta_block)[:, :, None])
        dscores_low = lax.optimization_barrier(dscores.astype(jnp.bfloat16)).astype(jnp.float32)
        grad_query_block = jnp.einsum('hqk,khd->qhd', dscores_low, key_heads) * score_scale
        key_total = key_total + jnp.einsum('hqk,qhd->khd', dscores_low, query_block) * score_scale
        value_total = value_total + jnp.einsum('hqk,qhd->khd', probs_low, grad_block)
        return ((key_total, value_total), grad_query_block.reshape(span, HDIM))
    start_carry = (jnp.zeros((TOKENS, H, HD), jnp.float32), jnp.zeros((TOKENS, H, HD), jnp.float32))
    (key_total, value_total), query_parts = lax.scan(one_step, start_carry, jnp.arange(count, dtype=jnp.int32))
    grad_query = query_parts.reshape(TOKENS, HDIM)
    return (grad_query, key_total.reshape(TOKENS, HDIM), value_total.reshape(TOKENS, HDIM))
```

```python
import functools
import math

import jax
import jax.numpy as jnp
from jax import lax
from jax.experimental import pallas as pl
from jax.experimental.pallas import tpu as pltpu
from jax.sharding import PartitionSpec as P

HD = 128
H = 4
MESH = pl.DeviceIdType.MESH
NT = (((1,), (1,)), ((), ()))
NN = (((1,), (0,)), ((), ()))
TN = (((0,), (0,)), ((), ()))
F32 = jnp.float32
BF16 = jnp.bfloat16
DROWS = 16
ARRIVAL = (0, 1, 3, 2)


def dot(a, b, dims):
    return lax.dot_general(a, b, dims, preferred_element_type=F32)


def kernel(
    n_qrow, n_kcol,
    order_ref, q_ref, k_ref, v_ref, lo_ref, go_ref, mask_ref,
    gq_ref, gk_ref, gv_ref,
    qs, gs, ks, vs, dbuf, p_buf, m_buf, c_buf, gqt,
    st, st_in, sa, ra, sib_out, sib_in, y_out, y_in, zk_out, zk_in, zq_out, zq_in,
    z_send, z_recv, aq_send, aq_recv, ag_send, ag_recv, bk_send, bk_recv, bv_send, bv_recv,
    s_send, s_recv, ga_send, ga_recv, sib_send, sib_recv, y_send, y_recv,
    zk_send, zk_recv, zq_send, zq_recv, own_sem,
):
    blk = q_ref.shape[0]
    n_a = (n_qrow // (2 * H)) * 2
    n_y = n_kcol // 2
    n_b = n_y * 2
    wide = H * blk
    scale = 1.0 / math.sqrt(HD)
    mq, mk = lax.axis_index("qrow"), lax.axis_index("kcol")
    core, z, r = mq % 2, (mq // 2) % H, mq // (2 * H)
    xb, y = mk % 2, mk // 2
    alpha = r * 2 + xb

    def z_of(d):
        return (z + d) % H

    def z_dev(d):
        return (r * (2 * H) + z_of(d) * 2 + core, mk)

    def a_dev(d):
        other = (alpha + d) % n_a
        return ((other // 2) * (2 * H) + z * 2 + core, y * 2 + other % 2)

    def y_dev(d):
        return (mq, ((y + d) % n_y) * 2 + xb)

    sibling = (r * (2 * H) + z * 2 + (core + 1) % 2, mk)

    def q_block(a, d):
        other = (alpha + a) % n_a
        return ((other // 2) * (2 * H) + z_of(d) * 2 + core) * n_kcol + y * 2 + other % 2

    def k_block(b, d):
        there = ((y + b // 2) % n_y) * 2 + xb
        return there * n_qrow + r * (2 * H) + z_of(d) * 2 + (core + b % 2) % 2

    def cols(d):
        return pl.ds(pl.multiple_of(z_of(d) * HD, HD), HD)

    def remote(src, dst, ss, rs, dev):
        return pltpu.make_async_remote_copy(
            src_ref=src, dst_ref=dst, send_sem=ss, recv_sem=rs, device_id=dev, device_id_type=MESH
        )

    barrier = pltpu.get_barrier_semaphore()
    partners = [z_dev(d) for d in range(1, H)]
    partners += [a_dev(d) for d in range(1, n_a)]
    partners += [y_dev(d) for d in range(1, n_y)] + [sibling]
    for dev in partners:
        pl.semaphore_signal(barrier, inc=1, device_id=dev, device_id_type=MESH)

    for h in range(H):
        at = slice(h * HD, (h + 1) * HD)
        prod = go_ref[:, at].astype(F32) * lo_ref[:, at].astype(F32)
        row = jnp.sum(prod.T, axis=0, keepdims=True)
        dbuf[h] = jnp.broadcast_to(row, (DROWS, blk)).astype(BF16)

    labels = lax.broadcasted_iota(jnp.int32, mask_ref.shape, 0)[:, :1]
    count = jnp.sum(mask_ref[...].astype(F32), axis=1, keepdims=True)
    first = labels.astype(F32) + 1.0 - count
    lane = lax.broadcasted_iota(jnp.int32, (1, blk), 1)

    def q_rows(a):
        pos, low = [], []
        for s in range(H):
            lb = order_ref[q_block(a, s)]
            pos.append(lb * blk + lane)
            f = jnp.sum(jnp.where(labels == lb, first, 0.0), axis=0, keepdims=True)
            low.append(jnp.broadcast_to(f, (1, blk)))
        return jnp.concatenate(pos, 1), jnp.concatenate(low, 1).astype(jnp.int32)

    key_iota = lax.broadcasted_iota(jnp.int32, (blk, wide), 0)
    q_pos = [q_rows(a) for a in range(n_a)]

    pl.semaphore_wait(barrier, len(partners))

    def z_pairs(d, e):
        at = cols(d)
        return [
            (q_ref.at[:, at], qs.at[0, e]),
            (k_ref.at[:, at], ks.at[0, e]),
            (go_ref.at[:, at], gs.at[0, e, pl.ds(0, blk)]),
            (dbuf.at[z_of(d)], gs.at[0, e, pl.ds(blk, DROWS)]),
            (v_ref.at[:, at], vs.at[0, e]),
        ]

    def z_copy(d, i):
        e = H - d
        src, dst = z_pairs(d, e)[i]
        return remote(src, dst, z_send.at[e, i], z_recv.at[e, i], z_dev(d))

    for group in ((0, 1), (2, 3, 4)):
        for d in (2, 1, 3):
            for i in group:
                z_copy(d, i).start()
    own = [
        pltpu.make_async_copy(src, dst, own_sem.at[i]) for i, (src, dst) in enumerate(z_pairs(0, 0))
    ]
    for copy in own:
        copy.start()

    def a_copy(buf, ss, rs, d, s):
        e = n_a - d
        return remote(buf.at[0, s], buf.at[e, s], ss.at[e, s], rs.at[e, s], a_dev(d))

    def y_copy(buf, ss, rs, d, s):
        e = 2 * (n_y - d)
        return remote(buf.at[0, s], buf.at[e, s], ss.at[e, s], rs.at[e, s], y_dev(d))

    def sib_copy(buf, ss, rs, d, s):
        e = 2 * d + 1
        return remote(buf.at[2 * d, s], buf.at[e, s], ss.at[e, s], rs.at[e, s], sibling)

    q_set, g_set = (qs, aq_send, aq_recv), (gs, ag_send, ag_recv)
    k_set, v_set = (ks, bk_send, bk_recv), (vs, bv_send, bv_recv)

    def forward(s, a_set, b_set, group):
        for i in group:
            if s == 0:
                own[i].wait()
            else:
                z_copy(H - s, i).wait_recv()
        for d in range(1, n_y):
            y_copy(*b_set, d, s).start()
        for d in range(1, n_a):
            a_copy(*a_set, d, s).start()
        sib_copy(*b_set, 0, s).start()

    def onward(b_set):
        for d in range(1, n_y):
            for s in ARRIVAL:
                y_copy(*b_set, n_y - d, s).wait_recv()
                sib_copy(*b_set, d, s).start()

    def wait_keys(b_set, b):
        if b % 2:
            for s in range(H):
                sib_copy(*b_set, b // 2, s).wait_recv()

    def wait_queries(a_set, a):
        if a:
            for s in range(H):
                a_copy(*a_set, n_a - a, s).wait_recv()

    def tile_scores(b, a):
        pos, low = q_pos[a]
        qa = qs[a].reshape(wide, HD)
        scores = dot(ks[b].reshape(wide, HD), qa, NT)
        for s in range(H):
            lb = order_ref[k_block(b, s)]
            limit = jnp.where(lb >= low, pos - lb * blk, -1)
            sc = jnp.where(key_iota <= limit, scores[s * blk : (s + 1) * blk] * scale, -1e30)
            m = jnp.max(sc, axis=0, keepdims=True)
            p = jnp.exp(sc - m)
            p_buf[a, b, s] = p
            m_buf[a, b, s] = m
            c_buf[a, b, s] = jnp.sum(p, axis=0, keepdims=True)

    for s in ARRIVAL:
        forward(s, q_set, k_set, (0, 1))
    forward(0, g_set, v_set, (2, 3, 4))
    later = [functools.partial(forward, s, g_set, v_set, (2, 3, 4)) for s in ARRIVAL[1:]]
    tile_scores(0, 0)
    onward(k_set)
    order = [(1, 0)] + [(b, a) for a in range(1, n_a) for b in (0, 1)]
    order += [(b, a) for b in range(2, n_b) for a in range(n_a)]
    ready_a, ready_b = {0}, {0}
    for b, a in order:
        if a not in ready_a:
            wait_queries(q_set, a)
            ready_a.add(a)
        if b not in ready_b:
            wait_keys(k_set, b)
            ready_b.add(b)
        tile_scores(b, a)
        if later:
            later.pop(0)()
    for rest in later:
        rest()

    for a in range(n_a):
        m_all = m_buf[a].reshape(n_b * H, wide)
        m = jnp.max(m_all, axis=0, keepdims=True)
        ls = c_buf[a].reshape(n_b * H, wide) * jnp.exp(m_all - m)
        st[a, 0:1] = m
        st[a, 1:2] = jnp.sum(ls, axis=0, keepdims=True)
        st[a, 2:8] = jnp.zeros((6, wide), F32)

    def s_copy(d):
        e = n_a - d
        return remote(st, st_in.at[e], s_send.at[e], s_recv.at[e], a_dev(d))

    for d in range(1, n_a):
        s_copy(d).start()
    onward(v_set)
    for a in range(1, n_a):
        wait_queries(g_set, a)
    for b in range(1, n_b):
        wait_keys(v_set, b)
    for d in range(1, n_a):
        s_copy(d).wait_recv()
    for a in range(n_a):
        m, l = st[a, 0:1], st[a, 1:2]
        for d in range(1, n_a):
            m2, l2 = st_in[d, (a - d) % n_a, 0:1], st_in[d, (a - d) % n_a, 1:2]
            top = jnp.maximum(m, m2)
            l = l * jnp.exp(m - top) + l2 * jnp.exp(m2 - top)
            m = top
        log_total = m + jnp.log(l)
        c_buf[a] = jnp.exp(m_buf[a] - log_total)

    def sib_sum(d, s):
        return remote(sib_out.at[d, s], sib_in.at[d, s], sib_send.at[d, s], sib_recv.at[d, s], sibling)

    def y_sum(d, s):
        e = n_y - d
        return remote(y_out.at[d, s], y_in.at[e, s], y_send.at[e, s], y_recv.at[e, s], y_dev(d))

    def zk_copy(d):
        e = H - d
        return remote(zk_out.at[d], zk_in.at[e], zk_send.at[e], zk_recv.at[e], z_dev(d))

    def zq_copy(d):
        e = H - d
        return remote(zq_out.at[d], zq_in.at[e], zq_send.at[e], zq_recv.at[e], z_dev(d))

    def ga_copy(d):
        e = n_a - d
        return remote(sa.at[d], ra.at[e], ga_send.at[e], ga_recv.at[e], a_dev(d))

    part = {}

    def compute(s, is_first):
        gk = gv = None
        for a in range(n_a):
            qa = qs[a].reshape(wide, HD)
            ga = gs[a, :, :blk, :].reshape(wide, HD)
            delta = jnp.concatenate([gs[a, t, blk : blk + DROWS, :][0:1].astype(F32) for t in range(H)], 1)
            dp = dot(vs[:, s].reshape(n_b * blk, HD), ga, NT)
            pr = (p_buf[a, :, s] * c_buf[a, :, s]).reshape(n_b * blk, wide)
            ds = (pr * (dp - delta)).astype(BF16)
            dk = dot(ds, qa, NN)
            dv = dot(pr.astype(BF16), ga, NN)
            gk = dk if a == 0 else gk + dk
            gv = dv if a == 0 else gv + dv
            term = dot(ks[:, s].reshape(n_b * blk, HD), ds, TN)
            gqt[a] = term if is_first else gqt[a] + term
        gk = gk * scale
        for d in range(n_y):
            mine = slice(2 * d * blk, (2 * d + 1) * blk)
            other = slice((2 * d + 1) * blk, (2 * d + 2) * blk)
            sib_out[d, s, 0] = gk[other].astype(BF16)
            sib_out[d, s, 1] = gv[other].astype(BF16)
            sib_sum(d, s).start()
            part[d, s] = [gk[mine], gv[mine]]

    def finish_y(s):
        for d in [*range(1, n_y), 0]:
            sib_sum(d, s).wait_recv()
            for i in range(2):
                part[d, s][i] = part[d, s][i] + sib_in[d, s, i].astype(F32)
            if d:
                for i in range(2):
                    y_out[d, s, i] = part[d, s][i].astype(BF16)
                y_sum(d, s).start()

    def finish_z(s):
        total = part[0, s]
        for d in range(1, n_y):
            y_sum(n_y - d, s).wait_recv()
            for i in range(2):
                total[i] = total[i] + y_in[d, s, i].astype(F32)
        if s:
            zk_out[s, 0] = total[0].astype(BF16)
            zk_out[s, 1] = total[1].astype(BF16)
            zk_copy(s).start()
        else:
            gk_ref[:, cols(0)] = total[0]
            gv_ref[:, cols(0)] = total[1]

    turns = (2, 1, 3, 0)
    for i, s in enumerate(turns):
        compute(s, i == 0)
        if i >= 1:
            finish_y(turns[i - 1])
        if i >= 2:
            finish_z(turns[i - 2])
    for a in range(1, n_a):
        sa[a] = (gqt[a].T * scale).astype(BF16).reshape(H, blk, HD)
        ga_copy(a).start()
    finish_y(turns[3])
    finish_z(turns[2])
    total_q = (gqt[0].T * scale).reshape(H, blk, HD)
    for d in range(1, n_a):
        ga_copy(n_a - d).wait_recv()
        total_q = total_q + ra[d].astype(F32)
    for d in (2, 1, 3):
        zq_out[d] = total_q[d].astype(BF16)
        zq_copy(d).start()
    gq_ref[:, cols(0)] = total_q[0]
    finish_z(turns[3])

    for d in (1, 3, 2):
        zk_copy(H - d).wait_recv()
        gk_ref[:, cols(d)] = zk_in[d, 0].astype(F32)
        gv_ref[:, cols(d)] = zk_in[d, 1].astype(F32)
    for d in (1, 3, 2):
        zq_copy(H - d).wait_recv()
        gq_ref[:, cols(d)] = zq_in[d].astype(F32)

    for d in range(1, H):
        for i in range(5):
            z_copy(d, i).wait_send()
        zk_copy(d).wait_send()
        zq_copy(d).wait_send()
    for d in range(1, n_a):
        for s in range(H):
            a_copy(*q_set, d, s).wait_send()
            a_copy(*g_set, d, s).wait_send()
        s_copy(d).wait_send()
        ga_copy(d).wait_send()
    for d in range(n_y):
        for s in range(H):
            sib_copy(*k_set, d, s).wait_send()
            sib_copy(*v_set, d, s).wait_send()
            sib_sum(d, s).wait_send()
            if d:
                y_copy(*k_set, d, s).wait_send()
                y_copy(*v_set, d, s).wait_send()
                y_sum(d, s).wait_send()


def body(n_qrow, n_kcol, query_rows, key_rows, value_rows, layer_out, grad_out, block_order, tile_mask):
    blk = query_rows.shape[0]
    n_a = (n_qrow // (2 * H)) * 2
    n_y = n_kcol // 2
    n_b = n_y * 2
    wide = H * blk
    vm = pl.BlockSpec(memory_space=pltpu.VMEM)
    sm = pl.BlockSpec(memory_space=pltpu.SMEM)
    dma = pltpu.SemaphoreType.DMA
    out = jax.ShapeDtypeStruct(query_rows.shape, F32)
    return pl.pallas_call(
        functools.partial(kernel, n_qrow, n_kcol),
        out_shape=(out, out, out),
        in_specs=[sm, vm, vm, vm, vm, vm, vm],
        out_specs=(vm, vm, vm),
        scratch_shapes=[
            pltpu.VMEM((n_a, H, blk, HD), BF16),
            pltpu.VMEM((n_a, H, blk + DROWS, HD), BF16),
            pltpu.VMEM((n_b, H, blk, HD), BF16),
            pltpu.VMEM((n_b, H, blk, HD), BF16),
            pltpu.VMEM((H, DROWS, blk), BF16),
            pltpu.VMEM((n_a, n_b, H, blk, wide), F32),
            pltpu.VMEM((n_a, n_b, H, 1, wide), F32),
            pltpu.VMEM((n_a, n_b, H, 1, wide), F32),
            pltpu.VMEM((n_a, HD, wide), F32),
            pltpu.VMEM((n_a, 8, wide), F32),
            pltpu.VMEM((n_a, n_a, 8, wide), F32),
            pltpu.VMEM((n_a, H, blk, HD), BF16),
            pltpu.VMEM((n_a, H, blk, HD), BF16),
            pltpu.VMEM((n_y, H, 2, blk, HD), BF16),
            pltpu.VMEM((n_y, H, 2, blk, HD), BF16),
            pltpu.VMEM((n_y, H, 2, blk, HD), BF16),
            pltpu.VMEM((n_y, H, 2, blk, HD), BF16),
            pltpu.VMEM((H, 2, blk, HD), BF16),
            pltpu.VMEM((H, 2, blk, HD), BF16),
            pltpu.VMEM((H, blk, HD), BF16),
            pltpu.VMEM((H, blk, HD), BF16),
            dma((H, 5)), dma((H, 5)),
            dma((n_a, H)), dma((n_a, H)),
            dma((n_a, H)), dma((n_a, H)),
            dma((n_b, H)), dma((n_b, H)),
            dma((n_b, H)), dma((n_b, H)),
            dma((n_a,)), dma((n_a,)),
            dma((n_a,)), dma((n_a,)),
            dma((n_y, H)), dma((n_y, H)),
            dma((n_y, H)), dma((n_y, H)),
            dma((H,)), dma((H,)),
            dma((H,)), dma((H,)),
            dma((5,)),
        ],
        compiler_params=pltpu.CompilerParams(
            collective_id=0, has_side_effects=True, vmem_limit_bytes=56 * 1024 * 1024
        ),
        name="attention_backward",
    )(block_order, query_rows, key_rows, value_rows, layer_out, grad_out, tile_mask)


def solution(mesh):
    rows = P(("qrow", "kcol"), None)
    keys = P(("kcol", "qrow"), None)
    return jax.shard_map(
        functools.partial(body, mesh.shape["qrow"], mesh.shape["kcol"]),
        mesh=mesh,
        in_specs=(rows, keys, keys, rows, rows, P(), P()),
        out_specs=(rows, keys, keys),
        check_vma=False,
    )
```

```python
import functools
import math

import jax
import jax.numpy as jnp
from jax import lax
from jax.experimental import pallas as pl
from jax.experimental.pallas import tpu as pltpu
from jax.sharding import PartitionSpec as P

HD = 128
H = 4
MESH = pl.DeviceIdType.MESH
NT = (((1,), (1,)), ((), ()))
NN = (((1,), (0,)), ((), ()))
TN = (((0,), (0,)), ((), ()))
F32 = jnp.float32
BF16 = jnp.bfloat16
DROWS = 16
ARRIVAL = (0, 1, 3, 2)


def dot(a, b, dims):
    return lax.dot_general(a, b, dims, preferred_element_type=F32)


def kernel(
    n_qrow, n_kcol,
    order_ref, q_ref, k_ref, v_ref, lo_ref, go_ref, mask_ref,
    gq_ref, gk_ref, gv_ref,
    qs, gs, ks, vs, dbuf, p_buf, m_buf, c_buf, gqt, acc,
    st, st_in, sa, ra, sib_out, sib_in, y_out, y_in, zk_out, zk_in, zq_out, zq_in,
    z_send, z_recv, aq_send, aq_recv, ag_send, ag_recv, bk_send, bk_recv, bv_send, bv_recv,
    s_send, s_recv, ga_send, ga_recv, sib_send, sib_recv, y_send, y_recv,
    zk_send, zk_recv, zq_send, zq_recv, own_sem,
):
    blk = q_ref.shape[0]
    n_a = (n_qrow // (2 * H)) * 2
    n_y = n_kcol // 2
    n_b = n_y * 2
    wide = H * blk
    scale = 1.0 / math.sqrt(HD)
    mq, mk = lax.axis_index("qrow"), lax.axis_index("kcol")
    core, z, r = mq % 2, (mq // 2) % H, mq // (2 * H)
    xb, y = mk % 2, mk // 2
    alpha = r * 2 + xb

    def z_of(d):
        return (z + d) % H

    def z_dev(d):
        return (r * (2 * H) + z_of(d) * 2 + core, mk)

    def a_dev(d):
        other = (alpha + d) % n_a
        return ((other // 2) * (2 * H) + z * 2 + core, y * 2 + other % 2)

    def y_dev(d):
        return (mq, ((y + d) % n_y) * 2 + xb)

    sibling = (r * (2 * H) + z * 2 + (core + 1) % 2, mk)

    def q_block(a, d):
        other = (alpha + a) % n_a
        return ((other // 2) * (2 * H) + z_of(d) * 2 + core) * n_kcol + y * 2 + other % 2

    def k_block(b, d):
        there = ((y + b // 2) % n_y) * 2 + xb
        return there * n_qrow + r * (2 * H) + z_of(d) * 2 + (core + b % 2) % 2

    def cols(d):
        return pl.ds(pl.multiple_of(z_of(d) * HD, HD), HD)

    def remote(src, dst, ss, rs, dev):
        return pltpu.make_async_remote_copy(
            src_ref=src, dst_ref=dst, send_sem=ss, recv_sem=rs, device_id=dev, device_id_type=MESH
        )

    barrier = pltpu.get_barrier_semaphore()
    partners = [z_dev(d) for d in range(1, H)]
    partners += [a_dev(d) for d in range(1, n_a)]
    partners += [y_dev(d) for d in range(1, n_y)] + [sibling]
    for dev in partners:
        pl.semaphore_signal(barrier, inc=1, device_id=dev, device_id_type=MESH)

    for h in range(H):
        at = slice(h * HD, (h + 1) * HD)
        prod = go_ref[:, at].astype(F32) * lo_ref[:, at].astype(F32)
        row = jnp.sum(prod.T, axis=0, keepdims=True)
        dbuf[h] = jnp.broadcast_to(row, (DROWS, blk)).astype(BF16)

    labels = lax.broadcasted_iota(jnp.int32, mask_ref.shape, 0)[:, :1]
    count = jnp.sum(mask_ref[...].astype(F32), axis=1, keepdims=True)
    first = labels.astype(F32) + 1.0 - count
    lane = lax.broadcasted_iota(jnp.int32, (1, blk), 1)

    def q_rows(a):
        pos, low = [], []
        for s in range(H):
            lb = order_ref[q_block(a, s)]
            pos.append(lb * blk + lane)
            f = jnp.sum(jnp.where(labels == lb, first, 0.0), axis=0, keepdims=True)
            low.append(jnp.broadcast_to(f, (1, blk)))
        return jnp.concatenate(pos, 1), jnp.concatenate(low, 1).astype(jnp.int32)

    key_iota = lax.broadcasted_iota(jnp.int32, (blk, wide), 0)
    q_pos = [q_rows(a) for a in range(n_a)]

    pl.semaphore_wait(barrier, len(partners))

    def z_pairs(d, e):
        at = cols(d)
        return [
            (q_ref.at[:, at], qs.at[0, e]),
            (k_ref.at[:, at], ks.at[0, e]),
            (go_ref.at[:, at], gs.at[0, e, pl.ds(0, blk)]),
            (dbuf.at[z_of(d)], gs.at[0, e, pl.ds(blk, DROWS)]),
            (v_ref.at[:, at], vs.at[0, e]),
        ]

    def z_copy(d, i):
        e = H - d
        src, dst = z_pairs(d, e)[i]
        return remote(src, dst, z_send.at[e, i], z_recv.at[e, i], z_dev(d))

    for group in ((0, 1), (2, 3, 4)):
        for d in (2, 1, 3):
            for i in group:
                z_copy(d, i).start()
    own = [
        pltpu.make_async_copy(src, dst, own_sem.at[i]) for i, (src, dst) in enumerate(z_pairs(0, 0))
    ]
    for copy in own:
        copy.start()

    def a_copy(buf, ss, rs, d, s):
        e = n_a - d
        return remote(buf.at[0, s], buf.at[e, s], ss.at[e, s], rs.at[e, s], a_dev(d))

    def y_copy(buf, ss, rs, d, s):
        e = 2 * (n_y - d)
        return remote(buf.at[0, s], buf.at[e, s], ss.at[e, s], rs.at[e, s], y_dev(d))

    def sib_copy(buf, ss, rs, d, s):
        e = 2 * d + 1
        return remote(buf.at[2 * d, s], buf.at[e, s], ss.at[e, s], rs.at[e, s], sibling)

    q_set, g_set = (qs, aq_send, aq_recv), (gs, ag_send, ag_recv)
    k_set, v_set = (ks, bk_send, bk_recv), (vs, bv_send, bv_recv)

    def forward(s, a_set, b_set, group):
        for i in group:
            if s == 0:
                own[i].wait()
            else:
                z_copy(H - s, i).wait_recv()
        for d in range(1, n_y):
            y_copy(*b_set, d, s).start()
        for d in range(1, n_a):
            a_copy(*a_set, d, s).start()
        sib_copy(*b_set, 0, s).start()

    def onward(b_set):
        for d in range(1, n_y):
            for s in ARRIVAL:
                y_copy(*b_set, n_y - d, s).wait_recv()
                sib_copy(*b_set, d, s).start()

    def wait_keys(b_set, b):
        if b % 2:
            for s in range(H):
                sib_copy(*b_set, b // 2, s).wait_recv()

    def wait_queries(a_set, a):
        if a:
            for s in range(H):
                a_copy(*a_set, n_a - a, s).wait_recv()

    def tile_scores(b, a):
        pos, low = q_pos[a]
        qa = qs[a].reshape(wide, HD)
        scores = dot(ks[b].reshape(wide, HD), qa, NT)
        for s in range(H):
            lb = order_ref[k_block(b, s)]
            limit = jnp.where(lb >= low, pos - lb * blk, -1)
            sc = jnp.where(key_iota <= limit, scores[s * blk : (s + 1) * blk] * scale, -1e30)
            m = jnp.max(sc, axis=0, keepdims=True)
            p = jnp.exp(sc - m)
            p_buf[a, b, s] = p
            m_buf[a, b, s] = m
            c_buf[a, b, s] = jnp.sum(p, axis=0, keepdims=True)

    for s in ARRIVAL:
        forward(s, q_set, k_set, (0, 1))
    forward(0, g_set, v_set, (2, 3, 4))
    later = [functools.partial(forward, s, g_set, v_set, (2, 3, 4)) for s in ARRIVAL[1:]]
    tile_scores(0, 0)
    onward(k_set)
    order = [(1, 0)] + [(b, a) for a in range(1, n_a) for b in (0, 1)]
    order += [(b, a) for b in range(2, n_b) for a in range(n_a)]
    ready_a, ready_b = {0}, {0}
    for b, a in order:
        if a not in ready_a:
            wait_queries(q_set, a)
            ready_a.add(a)
        if b not in ready_b:
            wait_keys(k_set, b)
            ready_b.add(b)
        tile_scores(b, a)
        if later:
            later.pop(0)()
    for rest in later:
        rest()

    for a in range(n_a):
        m_all = m_buf[a].reshape(n_b * H, wide)
        m = jnp.max(m_all, axis=0, keepdims=True)
        ls = c_buf[a].reshape(n_b * H, wide) * jnp.exp(m_all - m)
        st[a, 0:1] = m
        st[a, 1:2] = jnp.sum(ls, axis=0, keepdims=True)
        st[a, 2:8] = jnp.zeros((6, wide), F32)

    def s_copy(d):
        e = n_a - d
        return remote(st, st_in.at[e], s_send.at[e], s_recv.at[e], a_dev(d))

    turns = (2, 1, 3, 0)

    def queries(a):
        delta = jnp.concatenate([gs[a, t, blk : blk + DROWS, :][0:1].astype(F32) for t in range(H)], 1)
        return qs[a].reshape(wide, HD), gs[a, :, :blk, :].reshape(wide, HD), delta

    def dprobs(s, ga, delta):
        return dot(vs[:, s].reshape(n_b * blk, HD), ga, NT) - delta

    for d in range(1, n_a):
        s_copy(d).start()
    onward(v_set)
    for a in range(1, n_a):
        wait_queries(g_set, a)
    for b in range(1, n_b):
        wait_keys(v_set, b)
    _, last_g, last_delta = queries(n_a - 1)
    early = {s: dprobs(s, last_g, last_delta) for s in turns[:2]}
    for d in range(1, n_a):
        s_copy(d).wait_recv()
    for a in range(n_a):
        m, l = st[a, 0:1], st[a, 1:2]
        for d in range(1, n_a):
            m2, l2 = st_in[d, (a - d) % n_a, 0:1], st_in[d, (a - d) % n_a, 1:2]
            top = jnp.maximum(m, m2)
            l = l * jnp.exp(m - top) + l2 * jnp.exp(m2 - top)
            m = top
        log_total = m + jnp.log(l)
        c_buf[a] = jnp.exp(m_buf[a] - log_total)

    def sib_sum(d, s):
        return remote(sib_out.at[d, s], sib_in.at[d, s], sib_send.at[d, s], sib_recv.at[d, s], sibling)

    def y_sum(d, s):
        e = n_y - d
        return remote(y_out.at[d, s], y_in.at[e, s], y_send.at[e, s], y_recv.at[e, s], y_dev(d))

    def zk_copy(d):
        e = H - d
        return remote(zk_out.at[d], zk_in.at[e], zk_send.at[e], zk_recv.at[e], z_dev(d))

    def zq_copy(d):
        e = H - d
        return remote(zq_out.at[d], zq_in.at[e], zq_send.at[e], zq_recv.at[e], z_dev(d))

    def ga_copy(d):
        e = n_a - d
        return remote(sa.at[d], ra.at[e], ga_send.at[e], ga_recv.at[e], a_dev(d))

    part = {}
    def compute(a, s, early):
        qa, ga, delta = queries(a)
        dp = dprobs(s, ga, delta) if early is None else early
        pr = (p_buf[a, :, s] * c_buf[a, :, s]).reshape(n_b * blk, wide)
        ds = (pr * dp).astype(BF16)
        dk = dot(ds, qa, NN)
        dv = dot(pr.astype(BF16), ga, NN)
        term = dot(ks[:, s].reshape(n_b * blk, HD), ds, TN)
        gqt[a] = term if s == turns[0] else gqt[a] + term
        if a == n_a - 1:
            acc[s, 0], acc[s, 1] = dk, dv
            return
        if a:
            acc[s, 0] += dk
            acc[s, 1] += dv
            return
        gk = (acc[s, 0] + dk) * scale
        gv = acc[s, 1] + dv
        for d in range(n_y):
            mine = slice(2 * d * blk, (2 * d + 1) * blk)
            other = slice((2 * d + 1) * blk, (2 * d + 2) * blk)
            sib_out[d, s, 0] = gk[other].astype(BF16)
            sib_out[d, s, 1] = gv[other].astype(BF16)
            sib_sum(d, s).start()
            part[d, s] = [gk[mine], gv[mine]]

    def finish_y(s):
        for d in [*range(1, n_y), 0]:
            sib_sum(d, s).wait_recv()
            for i in range(2):
                part[d, s][i] = part[d, s][i] + sib_in[d, s, i].astype(F32)
            if d:
                for i in range(2):
                    y_out[d, s, i] = part[d, s][i].astype(BF16)
                y_sum(d, s).start()

    def finish_z(s):
        total = part[0, s]
        for d in range(1, n_y):
            y_sum(n_y - d, s).wait_recv()
            for i in range(2):
                total[i] = total[i] + y_in[d, s, i].astype(F32)
        if s:
            zk_out[s, 0] = total[0].astype(BF16)
            zk_out[s, 1] = total[1].astype(BF16)
            zk_copy(s).start()
        else:
            gk_ref[:, cols(0)] = total[0].astype(BF16)
            gv_ref[:, cols(0)] = total[1].astype(BF16)

    for a in range(n_a - 1, 0, -1):
        for s in turns:
            compute(a, s, early.get(s) if a == n_a - 1 else None)
        sa[a] = (gqt[a].T * scale).astype(BF16).reshape(H, blk, HD)
        ga_copy(a).start()
    for i, s in enumerate(turns):
        compute(0, s, None)
        if i >= 1:
            finish_y(turns[i - 1])
        if i >= 2:
            finish_z(turns[i - 2])
    total_q = (gqt[0].T * scale).reshape(H, blk, HD)
    for d in range(1, n_a):
        ga_copy(n_a - d).wait_recv()
        total_q = total_q + ra[d].astype(F32)
    for d in (2, 1, 3):
        zq_out[d] = total_q[d].astype(BF16)
        zq_copy(d).start()
    finish_y(turns[3])
    finish_z(turns[2])
    gq_ref[:, cols(0)] = total_q[0].astype(BF16)
    finish_z(turns[3])

    for d in (1, 3, 2):
        zk_copy(H - d).wait_recv()
        gk_ref[:, cols(d)] = zk_in[d, 0]
        gv_ref[:, cols(d)] = zk_in[d, 1]
    for d in (1, 3, 2):
        zq_copy(H - d).wait_recv()
        gq_ref[:, cols(d)] = zq_in[d]

    for d in range(1, H):
        for i in range(5):
            z_copy(d, i).wait_send()
        zk_copy(d).wait_send()
        zq_copy(d).wait_send()
    for d in range(1, n_a):
        for s in range(H):
            a_copy(*q_set, d, s).wait_send()
            a_copy(*g_set, d, s).wait_send()
        s_copy(d).wait_send()
        ga_copy(d).wait_send()
    for d in range(n_y):
        for s in range(H):
            sib_copy(*k_set, d, s).wait_send()
            sib_copy(*v_set, d, s).wait_send()
            sib_sum(d, s).wait_send()
            if d:
                y_copy(*k_set, d, s).wait_send()
                y_copy(*v_set, d, s).wait_send()
                y_sum(d, s).wait_send()


def body(n_qrow, n_kcol, query_rows, key_rows, value_rows, layer_out, grad_out, block_order, tile_mask):
    blk = query_rows.shape[0]
    n_a = (n_qrow // (2 * H)) * 2
    n_y = n_kcol // 2
    n_b = n_y * 2
    wide = H * blk
    vm = pl.BlockSpec(memory_space=pltpu.VMEM)
    sm = pl.BlockSpec(memory_space=pltpu.SMEM)
    dma = pltpu.SemaphoreType.DMA
    out = jax.ShapeDtypeStruct(query_rows.shape, BF16)
    grads = pl.pallas_call(
        functools.partial(kernel, n_qrow, n_kcol),
        out_shape=(out, out, out),
        in_specs=[sm, vm, vm, vm, vm, vm, vm],
        out_specs=(vm, vm, vm),
        scratch_shapes=[
            pltpu.VMEM((n_a, H, blk, HD), BF16),
            pltpu.VMEM((n_a, H, blk + DROWS, HD), BF16),
            pltpu.VMEM((n_b, H, blk, HD), BF16),
            pltpu.VMEM((n_b, H, blk, HD), BF16),
            pltpu.VMEM((H, DROWS, blk), BF16),
            pltpu.VMEM((n_a, n_b, H, blk, wide), F32),
            pltpu.VMEM((n_a, n_b, H, 1, wide), F32),
            pltpu.VMEM((n_a, n_b, H, 1, wide), F32),
            pltpu.VMEM((n_a, HD, wide), F32),
            pltpu.VMEM((H, 2, n_b * blk, HD), F32),
            pltpu.VMEM((n_a, 8, wide), F32),
            pltpu.VMEM((n_a, n_a, 8, wide), F32),
            pltpu.VMEM((n_a, H, blk, HD), BF16),
            pltpu.VMEM((n_a, H, blk, HD), BF16),
            pltpu.VMEM((n_y, H, 2, blk, HD), BF16),
            pltpu.VMEM((n_y, H, 2, blk, HD), BF16),
            pltpu.VMEM((n_y, H, 2, blk, HD), BF16),
            pltpu.VMEM((n_y, H, 2, blk, HD), BF16),
            pltpu.VMEM((H, 2, blk, HD), BF16),
            pltpu.VMEM((H, 2, blk, HD), BF16),
            pltpu.VMEM((H, blk, HD), BF16),
            pltpu.VMEM((H, blk, HD), BF16),
            dma((H, 5)), dma((H, 5)),
            dma((n_a, H)), dma((n_a, H)),
            dma((n_a, H)), dma((n_a, H)),
            dma((n_b, H)), dma((n_b, H)),
            dma((n_b, H)), dma((n_b, H)),
            dma((n_a,)), dma((n_a,)),
            dma((n_a,)), dma((n_a,)),
            dma((n_y, H)), dma((n_y, H)),
            dma((n_y, H)), dma((n_y, H)),
            dma((H,)), dma((H,)),
            dma((H,)), dma((H,)),
            dma((5,)),
        ],
        compiler_params=pltpu.CompilerParams(
            collective_id=0, has_side_effects=True, vmem_limit_bytes=56 * 1024 * 1024
        ),
        name="attention_backward",
    )(block_order, query_rows, key_rows, value_rows, layer_out, grad_out, tile_mask)
    return tuple(grad.astype(F32) for grad in grads)


def solution(mesh):
    rows = P(("qrow", "kcol"), None)
    keys = P(("kcol", "qrow"), None)
    return jax.shard_map(
        functools.partial(body, mesh.shape["qrow"], mesh.shape["kcol"]),
        mesh=mesh,
        in_specs=(rows, keys, keys, rows, rows, P(), P()),
        out_specs=(rows, keys, keys),
        check_vma=False,
    )
```

```python
import functools
import math

import jax
import jax.numpy as jnp
from jax import lax
from jax.experimental import pallas as pl
from jax.experimental.pallas import tpu as pltpu
from jax.sharding import PartitionSpec as P

HD = 128
H = 4
MESH = pl.DeviceIdType.MESH
NT = (((1,), (1,)), ((), ()))
NN = (((1,), (0,)), ((), ()))
TN = (((0,), (0,)), ((), ()))
F32 = jnp.float32
BF16 = jnp.bfloat16
DROWS = 16
ARRIVAL = (0, 1, 3, 2)


def dot(a, b, dims):
    return lax.dot_general(a, b, dims, preferred_element_type=F32)


def kernel(
    n_qrow, n_kcol,
    order_ref, q_ref, k_ref, v_ref, lo_ref, go_ref, mask_ref,
    gq_ref, gk_ref, gv_ref,
    qs, gs, ks, vs, dbuf, p_buf, m_buf, c_buf, gqt,
    st, st_in, sa, ra, sib_out, sib_in, y_out, y_in, zk_out, zk_in, zq_out, zq_in,
    z_send, z_recv, aq_send, aq_recv, ag_send, ag_recv, bk_send, bk_recv, bv_send, bv_recv,
    s_send, s_recv, ga_send, ga_recv, sib_send, sib_recv, y_send, y_recv,
    zk_send, zk_recv, zq_send, zq_recv, own_sem,
):
    blk = q_ref.shape[0]
    n_a = (n_qrow // (2 * H)) * 2
    n_y = n_kcol // 2
    n_b = n_y * 2
    wide = H * blk
    scale = 1.0 / math.sqrt(HD)
    mq, mk = lax.axis_index("qrow"), lax.axis_index("kcol")
    core, z, r = mq % 2, (mq // 2) % H, mq // (2 * H)
    xb, y = mk % 2, mk // 2
    alpha = r * 2 + xb

    def z_of(d):
        return (z + d) % H

    def z_dev(d):
        return (r * (2 * H) + z_of(d) * 2 + core, mk)

    def a_dev(d):
        other = (alpha + d) % n_a
        return ((other // 2) * (2 * H) + z * 2 + core, y * 2 + other % 2)

    def y_dev(d):
        return (mq, ((y + d) % n_y) * 2 + xb)

    sibling = (r * (2 * H) + z * 2 + (core + 1) % 2, mk)

    def q_block(a, d):
        other = (alpha + a) % n_a
        return ((other // 2) * (2 * H) + z_of(d) * 2 + core) * n_kcol + y * 2 + other % 2

    def k_block(b, d):
        there = ((y + b // 2) % n_y) * 2 + xb
        return there * n_qrow + r * (2 * H) + z_of(d) * 2 + (core + b % 2) % 2

    def cols(d):
        return pl.ds(pl.multiple_of(z_of(d) * HD, HD), HD)

    def remote(src, dst, ss, rs, dev):
        return pltpu.make_async_remote_copy(
            src_ref=src, dst_ref=dst, send_sem=ss, recv_sem=rs, device_id=dev, device_id_type=MESH
        )

    barrier = pltpu.get_barrier_semaphore()
    partners = [z_dev(d) for d in range(1, H)]
    partners += [a_dev(d) for d in range(1, n_a)]
    partners += [y_dev(d) for d in range(1, n_y)] + [sibling]
    for dev in partners:
        pl.semaphore_signal(barrier, inc=1, device_id=dev, device_id_type=MESH)

    for h in range(H):
        at = slice(h * HD, (h + 1) * HD)
        prod = go_ref[:, at].astype(F32) * lo_ref[:, at].astype(F32)
        row = jnp.sum(prod.T, axis=0, keepdims=True)
        dbuf[h] = jnp.broadcast_to(row, (DROWS, blk)).astype(BF16)

    labels = lax.broadcasted_iota(jnp.int32, mask_ref.shape, 0)[:, :1]
    count = jnp.sum(mask_ref[...].astype(F32), axis=1, keepdims=True)
    first = labels.astype(F32) + 1.0 - count
    lane = lax.broadcasted_iota(jnp.int32, (1, blk), 1)

    def q_rows(a):
        pos, low = [], []
        for s in range(H):
            lb = order_ref[q_block(a, s)]
            pos.append(lb * blk + lane)
            f = jnp.sum(jnp.where(labels == lb, first, 0.0), axis=0, keepdims=True)
            low.append(jnp.broadcast_to(f, (1, blk)))
        return jnp.concatenate(pos, 1), jnp.concatenate(low, 1).astype(jnp.int32)

    key_iota = lax.broadcasted_iota(jnp.int32, (blk, wide), 0)
    q_pos = [q_rows(a) for a in range(n_a)]

    pl.semaphore_wait(barrier, len(partners))

    def z_pairs(d, e):
        at = cols(d)
        return [
            (q_ref.at[:, at], qs.at[0, e]),
            (k_ref.at[:, at], ks.at[0, e]),
            (go_ref.at[:, at], gs.at[0, e, pl.ds(0, blk)]),
            (dbuf.at[z_of(d)], gs.at[0, e, pl.ds(blk, DROWS)]),
            (v_ref.at[:, at], vs.at[0, e]),
        ]

    def z_copy(d, i):
        e = H - d
        src, dst = z_pairs(d, e)[i]
        return remote(src, dst, z_send.at[e, i], z_recv.at[e, i], z_dev(d))

    for group in ((0, 1), (2, 3, 4)):
        for d in (2, 1, 3):
            for i in group:
                z_copy(d, i).start()
    own = [
        pltpu.make_async_copy(src, dst, own_sem.at[i]) for i, (src, dst) in enumerate(z_pairs(0, 0))
    ]
    for copy in own:
        copy.start()

    def a_copy(buf, ss, rs, d, s):
        e = n_a - d
        return remote(buf.at[0, s], buf.at[e, s], ss.at[e, s], rs.at[e, s], a_dev(d))

    def y_copy(buf, ss, rs, d, s):
        e = 2 * (n_y - d)
        return remote(buf.at[0, s], buf.at[e, s], ss.at[e, s], rs.at[e, s], y_dev(d))

    def sib_copy(buf, ss, rs, d, s):
        e = 2 * d + 1
        return remote(buf.at[2 * d, s], buf.at[e, s], ss.at[e, s], rs.at[e, s], sibling)

    q_set, g_set = (qs, aq_send, aq_recv), (gs, ag_send, ag_recv)
    k_set, v_set = (ks, bk_send, bk_recv), (vs, bv_send, bv_recv)

    def forward(s, a_set, b_set, group):
        for i in group:
            if s == 0:
                own[i].wait()
            else:
                z_copy(H - s, i).wait_recv()
        for d in range(1, n_y):
            y_copy(*b_set, d, s).start()
        for d in range(1, n_a):
            a_copy(*a_set, d, s).start()
        sib_copy(*b_set, 0, s).start()

    def onward(b_set):
        for d in range(1, n_y):
            for s in ARRIVAL:
                y_copy(*b_set, n_y - d, s).wait_recv()
                sib_copy(*b_set, d, s).start()

    def wait_keys(b_set, b):
        if b % 2:
            for s in range(H):
                sib_copy(*b_set, b // 2, s).wait_recv()

    def wait_queries(a_set, a):
        if a:
            for s in range(H):
                a_copy(*a_set, n_a - a, s).wait_recv()

    def tile_scores(b, a):
        pos, low = q_pos[a]
        qa = qs[a].reshape(wide, HD)
        scores = dot(ks[b].reshape(wide, HD), qa, NT)
        for s in range(H):
            lb = order_ref[k_block(b, s)]
            limit = jnp.where(lb >= low, pos - lb * blk, -1)
            sc = jnp.where(key_iota <= limit, scores[s * blk : (s + 1) * blk] * scale, -1e30)
            m = jnp.max(sc, axis=0, keepdims=True)
            p = jnp.exp(sc - m)
            p_buf[a, b, s] = p
            m_buf[a, b, s] = m
            c_buf[a, b, s] = jnp.sum(p, axis=0, keepdims=True)

    for s in ARRIVAL:
        forward(s, q_set, k_set, (0, 1))
    forward(0, g_set, v_set, (2, 3, 4))
    later = [functools.partial(forward, s, g_set, v_set, (2, 3, 4)) for s in ARRIVAL[1:]]
    tile_scores(0, 0)
    onward(k_set)
    order = [(1, 0)] + [(b, a) for a in range(1, n_a) for b in (0, 1)]
    order += [(b, a) for b in range(2, n_b) for a in range(n_a)]
    ready_a, ready_b = {0}, {0}
    for b, a in order:
        if a not in ready_a:
            wait_queries(q_set, a)
            ready_a.add(a)
        if b not in ready_b:
            wait_keys(k_set, b)
            ready_b.add(b)
        tile_scores(b, a)
        if later:
            later.pop(0)()
    for rest in later:
        rest()

    for a in range(n_a):
        m_all = m_buf[a].reshape(n_b * H, wide)
        m = jnp.max(m_all, axis=0, keepdims=True)
        ls = c_buf[a].reshape(n_b * H, wide) * jnp.exp(m_all - m)
        st[a, 0:1] = m
        st[a, 1:2] = jnp.sum(ls, axis=0, keepdims=True)
        st[a, 2:8] = jnp.zeros((6, wide), F32)

    def s_copy(d):
        e = n_a - d
        return remote(st, st_in.at[e], s_send.at[e], s_recv.at[e], a_dev(d))

    turns = (2, 1, 3, 0)

    def queries(a):
        delta = jnp.concatenate([gs[a, t, blk : blk + DROWS, :][0:1].astype(F32) for t in range(H)], 1)
        return qs[a].reshape(wide, HD), gs[a, :, :blk, :].reshape(wide, HD), delta

    def dprobs(s, ga, delta):
        return dot(vs[:, s].reshape(n_b * blk, HD), ga, NT) - delta

    for d in range(1, n_a):
        s_copy(d).start()
    onward(v_set)
    for a in range(1, n_a):
        wait_queries(g_set, a)
    for b in range(1, n_b):
        wait_keys(v_set, b)
    early = [dprobs(turns[0], *queries(a)[1:]) for a in range(n_a)]
    for d in range(1, n_a):
        s_copy(d).wait_recv()
    for a in range(n_a):
        m, l = st[a, 0:1], st[a, 1:2]
        for d in range(1, n_a):
            m2, l2 = st_in[d, (a - d) % n_a, 0:1], st_in[d, (a - d) % n_a, 1:2]
            top = jnp.maximum(m, m2)
            l = l * jnp.exp(m - top) + l2 * jnp.exp(m2 - top)
            m = top
        log_total = m + jnp.log(l)
        c_buf[a] = jnp.exp(m_buf[a] - log_total)

    def sib_sum(d, s):
        return remote(sib_out.at[d, s], sib_in.at[d, s], sib_send.at[d, s], sib_recv.at[d, s], sibling)

    def y_sum(d, s):
        e = n_y - d
        return remote(y_out.at[d, s], y_in.at[e, s], y_send.at[e, s], y_recv.at[e, s], y_dev(d))

    def zk_copy(d):
        e = H - d
        return remote(zk_out.at[d], zk_in.at[e], zk_send.at[e], zk_recv.at[e], z_dev(d))

    def zq_copy(d):
        e = H - d
        return remote(zq_out.at[d], zq_in.at[e], zq_send.at[e], zq_recv.at[e], z_dev(d))

    def ga_copy(d):
        e = n_a - d
        return remote(sa.at[d], ra.at[e], ga_send.at[e], ga_recv.at[e], a_dev(d))

    part = {}

    def compute(s, dps, is_last):
        gk = gv = None
        for a in range(n_a - 1, -1, -1):
            qa, ga, delta = queries(a)
            dp = dps[a] if dps else dprobs(s, ga, delta)
            pr = (p_buf[a, :, s] * c_buf[a, :, s]).reshape(n_b * blk, wide)
            ds = (pr * dp).astype(BF16)
            term = dot(ks[:, s].reshape(n_b * blk, HD), ds, TN)
            gqt[a] = term if dps else gqt[a] + term
            if is_last and a:
                sa[a] = (gqt[a].T * scale).astype(BF16).reshape(H, blk, HD)
                ga_copy(a).start()
            dk = dot(ds, qa, NN)
            dv = dot(pr.astype(BF16), ga, NN)
            gk = dk if gk is None else gk + dk
            gv = dv if gv is None else gv + dv
        gk = gk * scale
        for d in range(n_y):
            mine = slice(2 * d * blk, (2 * d + 1) * blk)
            other = slice((2 * d + 1) * blk, (2 * d + 2) * blk)
            sib_out[d, s, 0] = gk[other].astype(BF16)
            sib_out[d, s, 1] = gv[other].astype(BF16)
            sib_sum(d, s).start()
            part[d, s] = [gk[mine], gv[mine]]

    def finish_y(s):
        for d in [*range(1, n_y), 0]:
            sib_sum(d, s).wait_recv()
            for i in range(2):
                part[d, s][i] = part[d, s][i] + sib_in[d, s, i].astype(F32)
            if d:
                for i in range(2):
                    y_out[d, s, i] = part[d, s][i].astype(BF16)
                y_sum(d, s).start()

    def finish_z(s):
        total = part[0, s]
        for d in range(1, n_y):
            y_sum(n_y - d, s).wait_recv()
            for i in range(2):
                total[i] = total[i] + y_in[d, s, i].astype(F32)
        if s:
            zk_out[s, 0] = total[0].astype(BF16)
            zk_out[s, 1] = total[1].astype(BF16)
            zk_copy(s).start()
        else:
            gk_ref[:, cols(0)] = total[0]
            gv_ref[:, cols(0)] = total[1]

    for i, s in enumerate(turns):
        compute(s, early if i == 0 else None, i == H - 1)
        if i >= 1:
            finish_y(turns[i - 1])
        if i >= 2:
            finish_z(turns[i - 2])
    finish_y(turns[3])
    finish_z(turns[2])
    total_q = (gqt[0].T * scale).reshape(H, blk, HD)
    for d in range(1, n_a):
        ga_copy(n_a - d).wait_recv()
        total_q = total_q + ra[d].astype(F32)
    for d in (2, 1, 3):
        zq_out[d] = total_q[d].astype(BF16)
        zq_copy(d).start()
    gq_ref[:, cols(0)] = total_q[0]
    finish_z(turns[3])

    for d in (1, 3, 2):
        zk_copy(H - d).wait_recv()
        gk_ref[:, cols(d)] = zk_in[d, 0].astype(F32)
        gv_ref[:, cols(d)] = zk_in[d, 1].astype(F32)
    for d in (1, 3, 2):
        zq_copy(H - d).wait_recv()
        gq_ref[:, cols(d)] = zq_in[d].astype(F32)

    for d in range(1, H):
        for i in range(5):
            z_copy(d, i).wait_send()
        zk_copy(d).wait_send()
        zq_copy(d).wait_send()
    for d in range(1, n_a):
        for s in range(H):
            a_copy(*q_set, d, s).wait_send()
            a_copy(*g_set, d, s).wait_send()
        s_copy(d).wait_send()
        ga_copy(d).wait_send()
    for d in range(n_y):
        for s in range(H):
            sib_copy(*k_set, d, s).wait_send()
            sib_copy(*v_set, d, s).wait_send()
            sib_sum(d, s).wait_send()
            if d:
                y_copy(*k_set, d, s).wait_send()
                y_copy(*v_set, d, s).wait_send()
                y_sum(d, s).wait_send()


def hand_on(gq, gk, gv, gq_out, gk_out, gv_out, sem):
    copies = [
        pltpu.make_async_copy(src, dst, sem.at[i])
        for i, (src, dst) in enumerate([(gq, gq_out), (gk, gk_out), (gv, gv_out)])
    ]
    for copy in copies:
        copy.start()
    for copy in copies:
        copy.wait()


def body(n_qrow, n_kcol, query_rows, key_rows, value_rows, layer_out, grad_out, block_order, tile_mask):
    blk = query_rows.shape[0]
    n_a = (n_qrow // (2 * H)) * 2
    n_y = n_kcol // 2
    n_b = n_y * 2
    wide = H * blk
    vm = pl.BlockSpec(memory_space=pltpu.VMEM)
    sm = pl.BlockSpec(memory_space=pltpu.SMEM)
    dma = pltpu.SemaphoreType.DMA
    out = jax.ShapeDtypeStruct(query_rows.shape, F32)
    grads = pl.pallas_call(
        functools.partial(kernel, n_qrow, n_kcol),
        out_shape=(out, out, out),
        in_specs=[sm, vm, vm, vm, vm, vm, vm],
        out_specs=(vm, vm, vm),
        scratch_shapes=[
            pltpu.VMEM((n_a, H, blk, HD), BF16),
            pltpu.VMEM((n_a, H, blk + DROWS, HD), BF16),
            pltpu.VMEM((n_b, H, blk, HD), BF16),
            pltpu.VMEM((n_b, H, blk, HD), BF16),
            pltpu.VMEM((H, DROWS, blk), BF16),
            pltpu.VMEM((n_a, n_b, H, blk, wide), F32),
            pltpu.VMEM((n_a, n_b, H, 1, wide), F32),
            pltpu.VMEM((n_a, n_b, H, 1, wide), F32),
            pltpu.VMEM((n_a, HD, wide), F32),
            pltpu.VMEM((n_a, 8, wide), F32),
            pltpu.VMEM((n_a, n_a, 8, wide), F32),
            pltpu.VMEM((n_a, H, blk, HD), BF16),
            pltpu.VMEM((n_a, H, blk, HD), BF16),
            pltpu.VMEM((n_y, H, 2, blk, HD), BF16),
            pltpu.VMEM((n_y, H, 2, blk, HD), BF16),
            pltpu.VMEM((n_y, H, 2, blk, HD), BF16),
            pltpu.VMEM((n_y, H, 2, blk, HD), BF16),
            pltpu.VMEM((H, 2, blk, HD), BF16),
            pltpu.VMEM((H, 2, blk, HD), BF16),
            pltpu.VMEM((H, blk, HD), BF16),
            pltpu.VMEM((H, blk, HD), BF16),
            dma((H, 5)), dma((H, 5)),
            dma((n_a, H)), dma((n_a, H)),
            dma((n_a, H)), dma((n_a, H)),
            dma((n_b, H)), dma((n_b, H)),
            dma((n_b, H)), dma((n_b, H)),
            dma((n_a,)), dma((n_a,)),
            dma((n_a,)), dma((n_a,)),
            dma((n_y, H)), dma((n_y, H)),
            dma((n_y, H)), dma((n_y, H)),
            dma((H,)), dma((H,)),
            dma((H,)), dma((H,)),
            dma((5,)),
        ],
        compiler_params=pltpu.CompilerParams(
            collective_id=0, has_side_effects=True, vmem_limit_bytes=56 * 1024 * 1024
        ),
        name="attention_backward",
    )(block_order, query_rows, key_rows, value_rows, layer_out, grad_out, tile_mask)
    anywhere = pl.BlockSpec(memory_space=pl.ANY)
    return pl.pallas_call(
        hand_on,
        out_shape=(out, out, out),
        in_specs=[anywhere] * 3,
        out_specs=(anywhere,) * 3,
        scratch_shapes=[dma((3,))],
        name="hand_on",
    )(*grads)


def solution(mesh):
    rows = P(("qrow", "kcol"), None)
    keys = P(("kcol", "qrow"), None)
    return jax.shard_map(
        functools.partial(body, mesh.shape["qrow"], mesh.shape["kcol"]),
        mesh=mesh,
        in_specs=(rows, keys, keys, rows, rows, P(), P()),
        out_specs=(rows, keys, keys),
        check_vma=False,
    )
```
